32 devices in a mesh: space: 8 (over y, x, core), ifg: 4 (over z).
Axes of the slice: x: 2, y: 2, z: 4, core: 2. Of those that a mesh axis runs over, the one named last changes fastest.
Arguments:
- phases: float32 [192, 128, 1024], P('ifg', 'space'), may hold values from -12 to 12
- coherence: bfloat16 [192, 128, 1024], P('ifg', 'space'), may hold values from 0.19921875 to 1
- design: int32 [192, 2], replicated, may hold values from 0 to 99, as said below
- geo_lookup: int32 [256, 8], P(('space', 'ifg')), may hold values from -1 to 255, as said below
- geo_weights: bfloat16 [256, 8, 128, 128], P(('space', 'ifg')), may hold values from -0.25 to 0.25
Outputs:
- geo_series: float32 [256, 99, 128], P(('space', 'ifg'))
The draws below stay inside these ranges and needn't reach their ends.
Inputs may be any that keep to these rules, and one draw needn't show every extreme that they name: `design`: each row names two dates; the second is later than the first by 1 to 3 steps, and some row spans exactly 3. Rows are distinct and every pair of consecutive dates is a row. `geo_lookup`: an entry e >= 0 of a tile owned by device (o, g) names block e % 32 of the pixels that device (e // 32, g) holds after the regrouping; -1 marks an unused entry. Over all tiles of one device, at most 2 entries name blocks of one index of space, a number reached in every draw; in every group g one device's tiles name 2 blocks of every index of space.
All inputs are finite; a program needn't handle non-finite values.
Results may differ from the reference program's by a relative error of at most 0.0029.
Values may be sent and summed in bfloat16 or wider, within the bound.
A program may use at most 64 MiB of HBM per device.

```python
import jax
import jax.numpy as jnp
from jax import lax

IFGS = 192
DATES = 100
SPAN = 3
COLS = 1024
PASSES = 3
BLOCK = 128
TPX = 128
TILES_DEV = 8
J = 8
CAP = 2
SLAB_ROWS = 128
NBL = 32
BANDS = 8
GROUPS = 4
TILES = 256


def draw_design(key, part):
    cand_first = []
    cand_second = []
    for span_step in range(2, SPAN + 1):
        starts = jnp.arange(DATES - span_step, dtype=jnp.int32)
        cand_first.append(starts)
        cand_second.append(starts + span_step)
    cand_first = jnp.concatenate(cand_first)
    cand_second = jnp.concatenate(cand_second)
    cand_count = cand_first.shape[0]
    scores = jax.random.permutation(jax.random.fold_in(key, 11), cand_count).astype(jnp.int32)
    forced = (cand_first == 0) & (cand_second == SPAN)
    scores = jnp.where(forced, -1, scores)
    chosen = jnp.argsort(scores, stable=True)[:IFGS - DATES + 1]
    firsts = jnp.concatenate([jnp.arange(DATES - 1, dtype=jnp.int32), cand_first[chosen]])
    seconds = jnp.concatenate([jnp.arange(1, DATES, dtype=jnp.int32), cand_second[chosen]])
    shuffle = jax.random.permutation(jax.random.fold_in(key, 12), IFGS)
    return jnp.stack([firsts[shuffle], seconds[shuffle]], axis=1).astype(jnp.int32)


def draw_geo_lookup(key, part):
    owners = BANDS * GROUPS
    entries = TILES_DEV * J
    counts = jax.random.randint(jax.random.fold_in(key, 21), (owners, BANDS), 0, CAP + 1)
    forced_band = jax.random.randint(jax.random.fold_in(key, 22), (owners,), 0, BANDS)
    band_ids = jnp.arange(BANDS, dtype=jnp.int32)
    counts = jnp.where(band_ids[None, :] == forced_band[:, None], CAP, counts)
    full_owner = jax.random.randint(jax.random.fold_in(key, 23), (GROUPS,), 0, BANDS)
    owner_ids = jnp.arange(owners, dtype=jnp.int32)
    owner_band = owner_ids // GROUPS
    owner_group = owner_ids % GROUPS
    is_full = owner_band == full_owner[owner_group]
    counts = jnp.where(is_full[:, None], CAP, counts)
    bounds = jnp.cumsum(counts, axis=1)
    slot_index = jnp.arange(entries, dtype=jnp.int32)
    source = jnp.sum((bounds[:, None, :] <= slot_index[None, :, None]).astype(jnp.int32), axis=2)
    in_use = slot_index[None, :] < bounds[:, -1:]
    local_block = jax.random.randint(jax.random.fold_in(key, 24), (owners, entries), 0, NBL)
    block_ids = jnp.where(in_use, source * NBL + local_block, -1)
    owner_keys = jax.random.split(jax.random.fold_in(key, 25), owners)
    orders = jax.vmap(lambda k: jax.random.permutation(k, entries))(owner_keys)
    block_ids = jnp.take_along_axis(block_ids, orders, axis=1)
    return block_ids.reshape(owners * TILES_DEV, J).astype(jnp.int32)


def block_scale(stream_key, shape, pieces, low, high):
    loudness = 1.0
    for dim, blocks in pieces:
        steps = jax.random.uniform(jax.random.fold_in(jax.random.fold_in(stream_key, 6), dim), (blocks,), jnp.float32, low / len(pieces), high / len(pieces))
        loudness = loudness * jnp.repeat(jnp.exp(steps), shape[dim] // blocks).reshape((-1,) + (1,) * (len(shape) - 1 - dim))
    return loudness


def noise(stream_key, dims, scale, limit, pieces=(), kind=jnp.bfloat16):
    values = jax.random.normal(stream_key, dims, jnp.float32) * scale
    if len(pieces) > 0:
        values = block_scale(stream_key, dims, pieces, -0.22, 0.18) * values
    return jnp.clip(values, min=-limit, max=limit).astype(kind)


def setup_inputs(seed: int = 0) -> dict:
    arg_keys = jax.random.split(jax.random.key(seed), 6)
    return {
        "phases": noise(arg_keys[0], (IFGS, SLAB_ROWS, COLS), 2.0, 12.0, ((0, 4), (1, 8)), jnp.float32),
        "coherence": jnp.clip(0.19921875 + 0.80078125 * jax.random.uniform(arg_keys[1], (IFGS, SLAB_ROWS, COLS), jnp.float32) ** block_scale(arg_keys[1], (IFGS, SLAB_ROWS, COLS), ((0, 4), (1, 8)), -0.2, 0.2), 0.19921875, 1.0).astype(jnp.bfloat16),
        "design": draw_design(jax.random.fold_in(arg_keys[5], 71), 0),
        "geo_lookup": draw_geo_lookup(jax.random.fold_in(arg_keys[5], 71), 0),
        "geo_weights": noise(arg_keys[4], (TILES, J, BLOCK, TPX), (J * BLOCK // 2) ** -0.5, 0.25, ((0, 32),)),
    }


STEP_SIZE = 0.2
EDGE_SCALE = 2.0
SMOOTHING = 0.3
RIDGE_TERM = 0.2

def diffuse(extended, coh_extended, first_row, slab_rows):
    centre = extended[:, 1:-1]
    coh_middle = coh_extended[:, 1:-1]
    row_index = first_row + 1 + jnp.arange(centre.shape[1], dtype=jnp.int32)
    north_valid = (row_index >= 1).astype(jnp.float32)[None, :, None]
    south_valid = (row_index <= slab_rows - 2).astype(jnp.float32)[None, :, None]
    d_north = extended[:, :-2] - centre
    d_south = extended[:, 2:] - centre
    c_north = 0.5 * (coh_middle + coh_extended[:, :-2]) / (1.0 + d_north / EDGE_SCALE * (d_north / EDGE_SCALE))
    c_south = 0.5 * (coh_middle + coh_extended[:, 2:]) / (1.0 + d_south / EDGE_SCALE * (d_south / EDGE_SCALE))
    net_flux = north_valid * c_north * d_north + south_valid * c_south * d_south
    d_east = centre[:, :, 1:] - centre[:, :, :-1]
    east_coherence = 0.5 * (coh_middle[:, :, 1:] + coh_middle[:, :, :-1]) / (1.0 + d_east / EDGE_SCALE * (d_east / EDGE_SCALE))
    east_flux = east_coherence * d_east
    zero_col = jnp.zeros_like(centre[:, :, :1])
    net_flux = net_flux + jnp.concatenate([east_flux, zero_col], axis=2) - jnp.concatenate([zero_col, east_flux], axis=2)
    return centre + STEP_SIZE * net_flux

def build_design(design):
    unknown_dates = jnp.arange(1, DATES, dtype=jnp.int32)[None, :]
    later = (design[:, 1:2] == unknown_dates).astype(jnp.float32)
    earlier = (design[:, 0:1] == unknown_dates).astype(jnp.float32)
    return later - earlier

def normal_bands(design_f, weight_cols):
    unknowns = design_f.shape[1]
    row_ids = jnp.arange(unknowns - 1, dtype=jnp.int32)[:, None]
    col_ids = jnp.arange(unknowns, dtype=jnp.int32)[None, :]
    second = (col_ids == row_ids - 1).astype(jnp.float32) - 2.0 * (col_ids == row_ids).astype(jnp.float32) + (col_ids == row_ids + 1).astype(jnp.float32)
    smooth_gram = jnp.dot(second.T, second, precision=lax.Precision.HIGHEST)
    result = []
    for d in range(SPAN + 1):
        paired = design_f[:, :unknowns - d] * design_f[:, d:]
        data_term = jnp.dot(paired.T, weight_cols, precision=lax.Precision.HIGHEST)
        extra = SMOOTHING * jnp.diagonal(smooth_gram, d)
        if d == 0:
            extra = extra + RIDGE_TERM
        result.append(data_term + extra[:, None])
    return result

def solve_bands(normal, right_side):
    order_len = right_side.shape[0]
    factor = {}
    for j in range(order_len):
        running_total = normal[0][j]
        for k in range(max(0, j - SPAN), j):
            running_total = running_total - factor[j, k] * factor[j, k]
        diag_term = jnp.sqrt(running_total)
        factor[j, j] = diag_term
        for i in range(j + 1, min(order_len, j + SPAN + 1)):
            entry_sum = normal[i - j][j]
            for k in range(max(0, i - SPAN), j):
                entry_sum = entry_sum - factor[i, k] * factor[j, k]
            factor[i, j] = entry_sum / diag_term
    forward = []
    for j in range(order_len):
        entry_sum = right_side[j]
        for k in range(max(0, j - SPAN), j):
            entry_sum = entry_sum - factor[j, k] * forward[k]
        forward.append(entry_sum / factor[j, j])
    reverse_sweep = [None] * order_len
    for j in range(order_len - 1, -1, -1):
        entry_sum = forward[j]
        for i in range(j + 1, min(order_len, j + SPAN + 1)):
            entry_sum = entry_sum - factor[i, j] * reverse_sweep[i]
        reverse_sweep[j] = entry_sum / factor[j, j]
    return jnp.stack(reverse_sweep)

def reference(phases, coherence, design, geo_lookup, geo_weights):
    slab_rows = phases.shape[1]
    coherent = coherence.astype(jnp.float32)
    coh_padded = jnp.pad(coherent, ((0, 0), (1, 1), (0, 0)))
    current = phases
    for repeat in range(PASSES):
        extended = jnp.pad(current, ((0, 0), (1, 1), (0, 0)))
        current = diffuse(extended, coh_padded, -1, slab_rows)
    ifg_count = phases.shape[0]
    phase_cols = current.reshape(ifg_count, -1)
    weight_cols = coherent.reshape(ifg_count, -1)
    design_f = build_design(design)
    normal = normal_bands(design_f, weight_cols)
    right_side = jnp.dot(design_f.T, weight_cols * phase_cols, precision=lax.Precision.HIGHEST)
    series = solve_bands(normal, right_side).astype(jnp.bfloat16)
    unknowns = series.shape[0]
    blocks = series.reshape(unknowns, BANDS, GROUPS, NBL, BLOCK)
    owners = BANDS * GROUPS
    lists = geo_lookup.reshape(owners, TILES_DEV, J)
    matrices = geo_weights.reshape(owners, TILES_DEV, J, BLOCK, TPX)

    def one_owner(packed):
        owner, block_ids, weights_here = packed
        group = owner % GROUPS
        in_use = block_ids >= 0
        source = jnp.where(in_use, block_ids // NBL, 0)
        local_block = jnp.where(in_use, block_ids % NBL, 0)
        picked = blocks[:, source, group, local_block]
        picked = jnp.where(in_use[None, :, :, None], picked, jnp.zeros_like(picked))
        return jnp.einsum('utjp,tjpq->tuq', picked.astype(jnp.float32), weights_here.astype(jnp.float32), precision=lax.Precision.HIGHEST)
    result = lax.map(one_owner, (jnp.arange(owners, dtype=jnp.int32), lists, matrices))
    return result.reshape(owners * TILES_DEV, unknowns, TPX)
```

```python
import functools
import jax
import jax.numpy as jnp
from jax import lax
from jax.experimental import pallas as pl
from jax.experimental.pallas import tpu as pltpu
from jax.sharding import PartitionSpec as P

DATES = 100
SPAN = 3
PASSES = 3
BLOCK = 128
CAP = 2
STEP_SIZE = 0.2
SMOOTHING = 0.3
RIDGE_TERM = 0.2
SEND = jnp.float16


def diffuse_kernel(groups, lanes, u_ref, un_ref, us_ref, c_ref, cn_ref, cs_ref, d_out):
    band = lax.axis_index("space")
    last = lax.axis_size("space") - 1
    chunk, rows, cols = u_ref.shape
    total = rows + 8
    row = lax.broadcasted_iota(jnp.int32, (total, cols), 0)
    col = lax.broadcasted_iota(jnp.int32, (total, cols), 1)
    cut = ((row == total - 1) & (band == 0)) | ((row == rows - 1) & (band == last))
    vert = jnp.where(cut, 0.0, 0.5 * STEP_SIZE)
    east = jnp.where(col == cols - 1, 0.0, 0.5 * STEP_SIZE)
    gap = jnp.zeros((2, cols), jnp.float32)
    grows = rows // groups
    for k in range(chunk):
        u = jnp.concatenate([u_ref[k], us_ref[k], gap, un_ref[k]], axis=0)
        c = jnp.concatenate(
            [
                c_ref[k].astype(jnp.float32),
                cs_ref[k].astype(jnp.float32),
                gap,
                cn_ref[k].astype(jnp.float32),
            ],
            axis=0,
        )
        cv = vert * (c + pltpu.roll(c, total - 1, 0))
        ce = east * (c + pltpu.roll(c, cols - 1, 1))
        for _ in range(PASSES):
            dv = pltpu.roll(u, total - 1, 0) - u
            de = pltpu.roll(u, cols - 1, 1) - u
            fv = cv * dv / (1.0 + 0.25 * (dv * dv))
            fe = ce * de / (1.0 + 0.25 * (de * de))
            u = u + ((fv - pltpu.roll(fv, 1, 0)) + (fe - pltpu.roll(fe, 1, 1)))
        for g in range(groups):
            piece = u[g * grows : (g + 1) * grows]
            piece = jnp.concatenate(
                [piece[:, q * lanes : (q + 1) * lanes] for q in range(cols // lanes)], axis=0
            )
            d_out[g, k] = piece


def regroup_kernel(groups, lanes, c_ref, out):
    chunk, rows, cols = c_ref.shape
    grows = rows // groups
    for k in range(chunk):
        c = c_ref[k].astype(jnp.float32)
        for g in range(groups):
            piece = c[g * grows : (g + 1) * grows]
            piece = jnp.concatenate(
                [piece[:, q * lanes : (q + 1) * lanes] for q in range(cols // lanes)], axis=0
            )
            out[g, k] = piece.astype(out.dtype)


def solve_kernel(nslots, lanes, design, picks, w_ref, d_ref, out, table, low, total):
    ifgs, subs, _ = w_ref.shape
    unknowns = DATES - 1

    def clear(i, _):
        table[i] = -1
        return 0

    lax.fori_loop(0, SPAN * DATES, clear, 0)

    def fill(k, _):
        first = design[k, 0]
        table[(design[k, 1] - first - 1) * DATES + first] = k
        return 0

    lax.fori_loop(0, ifgs, fill, 0)

    def load(t):
        ws, wds = [], []
        for s in range(SPAN):
            k = table[s * DATES + t]
            used = k >= 0
            k = jnp.maximum(k, 0)
            w = jnp.where(used, w_ref[k].astype(jnp.float32), 0.0)
            ws.append(w)
            wds.append(w * d_ref[k].astype(jnp.float32))
        return ws, wds

    ws, wds = load(0)
    zero = ws[0] * 0.0

    def step(j, carry):
        d1, d2, d3, e1, e2, f1, b1, b2, b3 = carry
        (w1, w2, w3), (r1, r2, r3) = load(j + 1)
        diag = jnp.where(
            j == unknowns - 1, 1.0, jnp.where((j == 0) | (j == unknowns - 2), 5.0, 6.0)
        )
        first_off = jnp.where(j == unknowns - 2, -2.0, -4.0)
        a0 = d1 + (w1 + w2 + w3) + (SMOOTHING * diag + RIDGE_TERM)
        a1 = e1 - w1 + jnp.where(j == unknowns - 1, 0.0, SMOOTHING * first_off)
        a2 = f1 - w2 + jnp.where(j >= unknowns - 2, 0.0, SMOOTHING)
        a3 = -w3
        b = b1 - (r1 + r2 + r3)
        inv = 1.0 / a0
        l1, l2, l3 = a1 * inv, a2 * inv, a3 * inv
        low[j, 0], low[j, 1], low[j, 2] = l1, l2, l3
        low[j, 3] = b * inv
        return (
            (d2 + w1) - l1 * a1,
            (d3 + w2) - l2 * a2,
            w3 - l3 * a3,
            e2 - l1 * a2,
            -(l2 * a3),
            -(l1 * a3),
            (b2 + r1) - l1 * b,
            (b3 + r2) - l2 * b,
            r3 - l3 * b,
        )

    lax.fori_loop(0, unknowns, step, (*ws, zero, zero, zero, *wds))

    def back(i, carry):
        x1, x2, x3 = carry
        j = unknowns - 1 - i
        x = low[j, 3] - low[j, 2] * x3 - low[j, 1] * x2 - low[j, 0] * x1
        for q in range(lanes // BLOCK):
            total[q, pl.ds(pl.multiple_of(j * subs, 8), subs), :] = x[
                :, q * BLOCK : (q + 1) * BLOCK
            ]
        return x, x1, x2

    lax.fori_loop(0, unknowns, back, (zero, zero, zero))

    for s in range(nslots):
        row = picks[s, 0]
        tile = picks[s, 1]
        out[s] = total[tile, pl.ds(row, unknowns, stride=subs), :].astype(out.dtype)


def geo_kernel(width, slots, blocks, weights, out):
    t = pl.program_id(0)
    acc = jnp.zeros(out.shape[1:], jnp.float32)
    for j in range(width):
        slot = slots[t * width + j]
        block = blocks[jnp.maximum(slot, 0)]
        block = jnp.where(slot >= 0, block, jnp.zeros_like(block))
        acc = acc + jnp.dot(block, weights[0, j], preferred_element_type=jnp.float32)
    out[0] = acc


def per_device(phases, coherence, design, geo_lookup, geo_weights):
    bands = lax.axis_size("space")
    groups = lax.axis_size("ifg")
    ifgs, rows, cols = phases.shape
    band = lax.axis_index("space")
    unknowns = DATES - 1
    pixels = rows * cols // groups
    nbl = pixels // BLOCK
    lanes = min(256, pixels // 8)
    subs = pixels // lanes
    grows = rows // groups
    tiles, width = geo_lookup.shape

    own = geo_lookup.reshape(1, -1)
    lists = lax.all_gather(own, "space", axis=0, tiled=True)
    entries = lists.shape[1]
    order = jnp.arange(entries, dtype=jnp.int32)
    earlier = order[None, :] < order[:, None]
    mine = (lists >= band * nbl) & (lists < (band + 1) * nbl)
    rank = jnp.sum((mine[:, None, :] & earlier[None]).astype(jnp.int32), axis=2)
    chosen = mine[:, None, :] & (rank[:, None, :] == jnp.arange(CAP, dtype=jnp.int32)[None, :, None])
    picked = jnp.sum(jnp.where(chosen, (lists % nbl)[:, None, :], 0), axis=2).reshape(-1)
    tiles_row = cols // BLOCK
    tiles_lane = lanes // BLOCK
    place = picked % tiles_row
    picks = jnp.stack(
        [picked // tiles_row + grows * (place // tiles_lane), place % tiles_lane], axis=1
    )
    source = jnp.where(own[0] >= 0, own[0] // nbl, -1)
    same = (source[None, :] == source[:, None]) & earlier
    slots = jnp.where(
        own[0] >= 0, source * CAP + jnp.sum(same.astype(jnp.int32), axis=1), -1
    )

    down = [(i, i + 1) for i in range(bands - 1)]
    up = [(i + 1, i) for i in range(bands - 1)]
    cn = lax.ppermute(coherence[:, rows - PASSES :], "space", down)
    cs = lax.ppermute(coherence[:, :PASSES], "space", up)
    un = lax.ppermute(phases[:, rows - PASSES :], "space", down)
    us = lax.ppermute(phases[:, :PASSES], "space", up)

    chunk = 4
    whole = pl.BlockSpec((chunk, rows, cols), lambda i: (i, 0, 0))
    edge = pl.BlockSpec((chunk, PASSES, cols), lambda i: (i, 0, 0))
    regrouped = pl.BlockSpec((groups, chunk, subs, lanes), lambda i: (0, i, 0, 0))
    weights_g = pl.pallas_call(
        functools.partial(regroup_kernel, groups, lanes),
        grid=(ifgs // chunk,),
        in_specs=[whole],
        out_specs=regrouped,
        out_shape=jax.ShapeDtypeStruct((groups, ifgs, subs, lanes), jnp.bfloat16),
        name="regroup",
    )(coherence)
    diffused = pl.pallas_call(
        functools.partial(diffuse_kernel, groups, lanes),
        grid=(ifgs // chunk,),
        in_specs=[whole, edge, edge, whole, edge, edge],
        out_specs=regrouped,
        out_shape=jax.ShapeDtypeStruct((groups, ifgs, subs, lanes), jnp.float32),
        cost_estimate=pl.CostEstimate(
            flops=100 * ifgs * rows * cols, bytes_accessed=10**7, transcendentals=0
        ),
        name="diffuse",
    )(phases, un, us, coherence, cn, cs)
    w = lax.all_to_all(weights_g, "ifg", 0, 0, tiled=True).reshape(-1, subs, lanes)
    d = lax.all_to_all(diffused.astype(SEND), "ifg", 0, 0, tiled=True).reshape(-1, subs, lanes)
    d = d.astype(jnp.float32)

    nslots = bands * CAP
    vmem = pl.BlockSpec(memory_space=pltpu.VMEM)
    smem = pl.BlockSpec(memory_space=pltpu.SMEM)
    send = pl.pallas_call(
        functools.partial(solve_kernel, nslots, lanes),
        in_specs=[smem, smem, vmem, vmem],
        out_specs=vmem,
        out_shape=jax.ShapeDtypeStruct((nslots, unknowns, BLOCK), jnp.bfloat16),
        scratch_shapes=[
            pltpu.SMEM((SPAN * DATES,), jnp.int32),
            pltpu.VMEM((unknowns, 4, subs, lanes), jnp.float32),
            pltpu.VMEM((lanes // BLOCK, unknowns * subs, BLOCK), jnp.float32),
        ],
        compiler_params=pltpu.CompilerParams(vmem_limit_bytes=32 * 2**20),
        name="solve",
    )(design, picks, w, d)
    got = lax.all_to_all(send, "space", 0, 0, tiled=True)

    return pl.pallas_call(
        functools.partial(geo_kernel, width),
        grid_spec=pltpu.PrefetchScalarGridSpec(
            num_scalar_prefetch=1,
            grid=(tiles,),
            in_specs=[
                pl.BlockSpec((nslots, unknowns, BLOCK), lambda t, s: (0, 0, 0)),
                pl.BlockSpec((1, width, BLOCK, geo_weights.shape[3]), lambda t, s: (t, 0, 0, 0)),
            ],
            out_specs=pl.BlockSpec((1, unknowns, geo_weights.shape[3]), lambda t, s: (t, 0, 0)),
        ),
        out_shape=jax.ShapeDtypeStruct((tiles, unknowns, geo_weights.shape[3]), jnp.float32),
        name="geo",
    )(slots, got, geo_weights)


def solution(mesh):
    placed = (
        P("ifg", "space", None),
        P("ifg", "space", None),
        P(),
        P(("space", "ifg"), None),
        P(("space", "ifg"), None, None, None),
    )
    return jax.shard_map(
        per_device,
        mesh=mesh,
        in_specs=placed,
        out_specs=P(("space", "ifg"), None, None),
        check_vma=False,
    )
```

```python
import functools
import jax
import jax.numpy as jnp
from jax import lax
from jax.experimental import pallas as pl
from jax.experimental.pallas import tpu as pltpu
from jax.sharding import PartitionSpec as P

DATES = 100
SPAN = 3
PASSES = 3
BLOCK = 128
CAP = 2
STEP_SIZE = 0.2
SMOOTHING = 0.3
RIDGE_TERM = 0.2
OCTAVE = 1280.0
FLOOR = 21.9
UNROLL = 4
MESH = pl.DeviceIdType.MESH


def encode(u):
    size = (jnp.log2(jnp.maximum(jnp.abs(u), 1e-30)) + FLOOR) * OCTAVE + 0.5
    code = jnp.clip(size, 0.0, 32767.0).astype(jnp.int32)
    return jnp.where(u < 0, -code, code).astype(jnp.int16)


def decode(code):
    code = code.astype(jnp.int32).astype(jnp.float32)
    size = jnp.exp2(jnp.abs(code) * (1.0 / OCTAVE) - FLOOR)
    return jnp.where(code > 0, size, jnp.where(code < 0, -size, 0.0))


def lists_kernel(own_ref, out, send_sem, recv_sem, own_sem):
    groups = lax.axis_size("ifg")
    count = lax.axis_size("space") * groups
    me = lax.axis_index("space") * groups + lax.axis_index("ifg")
    barrier = pltpu.get_barrier_semaphore()

    def greet(r, _):
        peer = lax.rem(me + r, count)
        pl.semaphore_signal(
            barrier, inc=1, device_id=(peer // groups, lax.rem(peer, groups)), device_id_type=MESH
        )
        return 0

    lax.fori_loop(1, count, greet, 0)
    pl.semaphore_wait(barrier, count - 1)

    def send(r, _):
        peer = lax.rem(me + r, count)
        pltpu.make_async_remote_copy(
            src_ref=own_ref.at[0],
            dst_ref=out.at[me],
            send_sem=send_sem,
            recv_sem=recv_sem,
            device_id=(peer // groups, lax.rem(peer, groups)),
            device_id_type=MESH,
        ).start()
        return 0

    lax.fori_loop(1, count, send, 0)
    mine = pltpu.make_async_copy(own_ref.at[0], out.at[me], own_sem)
    mine.start()
    mine.wait()
    rest = out.at[pl.ds(0, count - 1)]
    landed = pltpu.make_async_remote_copy(
        src_ref=rest,
        dst_ref=rest,
        send_sem=send_sem,
        recv_sem=recv_sem,
        device_id=(lax.rem(me + 1, count) // groups, lax.rem(me + 1, groups)),
        device_id_type=MESH,
    )
    landed.wait_send()
    landed.wait_recv()


def spread_kernel(
    u_ref, un_ref, us_ref, c_ref, cn_ref, cs_ref, sel_ref, w_out, d_out,
    w_send, d_send, send_w, recv_w, send_d, recv_d, own_sem,
):
    band = lax.axis_index("space")
    last = lax.axis_size("space") - 1
    me = lax.axis_index("ifg")
    groups = lax.axis_size("ifg")
    ifgs, rows, cols = u_ref.shape
    slots = w_out.shape[2]
    barrier = pltpu.get_barrier_semaphore()
    peers = [lax.rem(me + r, groups) for r in range(groups)]
    for r in range(1, groups):
        pl.semaphore_signal(barrier, inc=1, device_id=(band, peers[r]), device_id_type=MESH)
    pl.semaphore_wait(barrier, groups - 1)

    def push(src, dst, span, send_sem, recv_sem, r):
        return pltpu.make_async_remote_copy(
            src_ref=src.at[peers[r], span],
            dst_ref=dst.at[me, span],
            send_sem=send_sem.at[r],
            recv_sem=recv_sem.at[r],
            device_id=(band, peers[r]),
            device_id_type=MESH,
        )

    def tiles(x):
        return jnp.concatenate(
            [x[:, q * BLOCK : (q + 1) * BLOCK] for q in range(cols // BLOCK)], axis=0
        )

    def pick(x):
        return jnp.dot(sel_ref[...], x, preferred_element_type=jnp.float32)

    def weigh(i, _):
        for kk in range(UNROLL):
            k = i * UNROLL + kk
            got = pick(tiles(c_ref[k]))
            for g in range(groups):
                w_send[g, k] = got[g * slots : (g + 1) * slots].astype(w_send.dtype)
        return 0

    lax.fori_loop(0, ifgs // UNROLL, weigh, 0)
    everything = pl.ds(0, ifgs)
    for r in range(1, groups):
        push(w_send, w_out, everything, send_w, recv_w, r).start()
    own_w = pltpu.make_async_copy(w_send.at[me], w_out.at[me], own_sem.at[0])
    own_w.start()

    total = rows + 8
    row = lax.broadcasted_iota(jnp.int32, (total, cols), 0)
    col = lax.broadcasted_iota(jnp.int32, (total, cols), 1)
    cut = ((row == total - 1) & (band == 0)) | ((row == rows - 1) & (band == last))
    vert = jnp.where(cut, 0.0, 0.5 * STEP_SIZE)
    east = jnp.where(col == cols - 1, 0.0, 0.5 * STEP_SIZE)
    gap = jnp.zeros((2, cols), jnp.float32)

    def diffuse(i, _):
        for kk in range(UNROLL):
            k = i * UNROLL + kk
            u = jnp.concatenate([u_ref[k], us_ref[k], gap, un_ref[k]], axis=0)
            c = jnp.concatenate(
                [
                    c_ref[k].astype(jnp.float32),
                    cs_ref[k].astype(jnp.float32),
                    gap,
                    cn_ref[k].astype(jnp.float32),
                ],
                axis=0,
            )
            cv = vert * (c + pltpu.roll(c, total - 1, 0))
            ce = east * (c + pltpu.roll(c, cols - 1, 1))
            for _ in range(PASSES):
                dv = pltpu.roll(u, total - 1, 0) - u
                de = pltpu.roll(u, cols - 1, 1) - u
                fv = cv * dv / (1.0 + 0.25 * (dv * dv))
                fe = ce * de / (1.0 + 0.25 * (de * de))
                u = u + ((fv - pltpu.roll(fv, 1, 0)) + (fe - pltpu.roll(fe, 1, 1)))
            u = tiles(u[:rows])
            high = u.astype(jnp.bfloat16)
            got = pick(high) + pick((u - high.astype(jnp.float32)).astype(jnp.bfloat16))
            for g in range(groups):
                d_send[g, k] = encode(got[g * slots : (g + 1) * slots])
        for r in range(1, groups):
            push(d_send, d_out, pl.ds(i * UNROLL, UNROLL), send_d, recv_d, r).start()
        return 0

    lax.fori_loop(0, ifgs // UNROLL, diffuse, 0)
    own_d = pltpu.make_async_copy(d_send.at[me], d_out.at[me], own_sem.at[1])
    own_d.start()
    own_w.wait()
    own_d.wait()
    for r in range(1, groups):
        push(w_send, w_out, everything, send_w, recv_w, r).wait()
        push(d_send, d_out, everything, send_d, recv_d, r).wait()


def solve_kernel(design, w_ref, d_ref, out, table, low, total):
    ifgs, subs, lanes = w_ref.shape
    unknowns = DATES - 1

    def clear(i, _):
        table[i] = -1
        return 0

    lax.fori_loop(0, SPAN * DATES, clear, 0)

    def fill(k, _):
        first = design[k, 0]
        table[(design[k, 1] - first - 1) * DATES + first] = k
        return 0

    lax.fori_loop(0, ifgs, fill, 0)

    def load(t):
        ws, wds = [], []
        for s in range(SPAN):
            k = table[s * DATES + t]
            used = k >= 0
            k = jnp.maximum(k, 0)
            w = jnp.where(used, w_ref[k].astype(jnp.float32), 0.0)
            ws.append(w)
            wds.append(w * decode(d_ref[k]))
        return ws, wds

    ws, wds = load(0)
    zero = ws[0] * 0.0

    def step(j, carry):
        d1, d2, d3, e1, e2, f1, b1, b2, b3 = carry
        (w1, w2, w3), (r1, r2, r3) = load(j + 1)
        diag = jnp.where(
            j == unknowns - 1, 1.0, jnp.where((j == 0) | (j == unknowns - 2), 5.0, 6.0)
        )
        first_off = jnp.where(j == unknowns - 2, -2.0, -4.0)
        a0 = d1 + (w1 + w2 + w3) + (SMOOTHING * diag + RIDGE_TERM)
        a1 = e1 - w1 + jnp.where(j == unknowns - 1, 0.0, SMOOTHING * first_off)
        a2 = f1 - w2 + jnp.where(j >= unknowns - 2, 0.0, SMOOTHING)
        a3 = -w3
        b = b1 - (r1 + r2 + r3)
        inv = 1.0 / a0
        l1, l2, l3 = a1 * inv, a2 * inv, a3 * inv
        low[j, 0], low[j, 1], low[j, 2] = l1, l2, l3
        low[j, 3] = b * inv
        return (
            (d2 + w1) - l1 * a1,
            (d3 + w2) - l2 * a2,
            w3 - l3 * a3,
            e2 - l1 * a2,
            -(l2 * a3),
            -(l1 * a3),
            (b2 + r1) - l1 * b,
            (b3 + r2) - l2 * b,
            r3 - l3 * b,
        )

    lax.fori_loop(0, unknowns, step, (*ws, zero, zero, zero, *wds))

    def back(i, carry):
        x1, x2, x3 = carry
        j = unknowns - 1 - i
        x = low[j, 3] - low[j, 2] * x3 - low[j, 1] * x2 - low[j, 0] * x1
        total[pl.ds(pl.multiple_of(j * subs, 8), subs), :] = x
        return x, x1, x2

    total[pl.ds(unknowns * subs, (out.shape[1] - unknowns) * subs), :] = jnp.zeros(
        ((out.shape[1] - unknowns) * subs, lanes), jnp.float32
    )
    lax.fori_loop(0, unknowns, back, (zero, zero, zero))
    for s in range(subs):
        out[s] = total[pl.ds(s, out.shape[1], stride=subs), :].astype(out.dtype)


def geo_kernel(width, slots, send, weights, out, blocks, send_sem, recv_sem, own_sem):
    bands = lax.axis_size("space")
    me = lax.axis_index("space")
    group = lax.axis_index("ifg")
    barrier = pltpu.get_barrier_semaphore()
    peers = [lax.rem(me + r, bands) for r in range(bands)]
    for r in range(1, bands):
        pl.semaphore_signal(barrier, inc=1, device_id=(peers[r], group), device_id_type=MESH)
    pl.semaphore_wait(barrier, bands - 1)
    copies = [
        pltpu.make_async_remote_copy(
            src_ref=send.at[pl.ds(peers[r] * CAP, CAP)],
            dst_ref=blocks.at[pl.ds(me * CAP, CAP)],
            send_sem=send_sem.at[r],
            recv_sem=recv_sem.at[r],
            device_id=(peers[r], group),
            device_id_type=MESH,
        )
        for r in range(1, bands)
    ]
    for copy in copies:
        copy.start()
    own = pltpu.make_async_copy(
        send.at[pl.ds(me * CAP, CAP)], blocks.at[pl.ds(me * CAP, CAP)], own_sem
    )
    own.start()
    own.wait()
    for copy in copies:
        copy.wait()
    for t in range(out.shape[0]):
        acc = jnp.zeros((blocks.shape[1], out.shape[2]), jnp.float32)
        for j in range(width):
            slot = slots[t * width + j]
            block = blocks[jnp.maximum(slot, 0)]
            block = jnp.where(slot >= 0, block, jnp.zeros_like(block))
            acc = acc + jnp.dot(block, weights[t, j], preferred_element_type=jnp.float32)
        out[t] = acc[: out.shape[1]]


def per_device(phases, coherence, design, geo_lookup, geo_weights):
    bands = lax.axis_size("space")
    groups = lax.axis_size("ifg")
    ifgs, rows, cols = phases.shape
    band = lax.axis_index("space")
    unknowns = DATES - 1
    padded = (unknowns + 15) // 16 * 16
    pixels = rows * cols // groups
    nbl = pixels // BLOCK
    grows = rows // groups
    tiles, width = geo_lookup.shape
    entries = tiles * width
    nslots = bands * CAP
    vmem = pl.BlockSpec(memory_space=pltpu.VMEM)
    smem = pl.BlockSpec(memory_space=pltpu.SMEM)
    dma = pltpu.SemaphoreType.DMA

    down = [(i, i + 1) for i in range(bands - 1)]
    up = [(i + 1, i) for i in range(bands - 1)]
    cn = lax.ppermute(coherence[:, rows - PASSES :], "space", down)
    cs = lax.ppermute(coherence[:, :PASSES], "space", up)
    un = lax.ppermute(phases[:, rows - PASSES :], "space", down)
    us = lax.ppermute(phases[:, :PASSES], "space", up)

    own = geo_lookup.reshape(-1)
    lists = pl.pallas_call(
        lists_kernel,
        in_specs=[vmem],
        out_specs=vmem,
        out_shape=jax.ShapeDtypeStruct((bands * groups, 8, BLOCK), jnp.int32),
        scratch_shapes=[dma, dma, dma],
        compiler_params=pltpu.CompilerParams(collective_id=0, has_side_effects=True),
        name="lists",
    )(jnp.broadcast_to(jnp.pad(own, (0, BLOCK - entries)), (1, 8, BLOCK)))
    lists = lists[:, 0, :entries].reshape(bands, groups, entries).transpose(1, 0, 2)
    order = jnp.arange(entries, dtype=jnp.int32)
    earlier = order[None, :] < order[:, None]
    mine = (lists >= band * nbl) & (lists < (band + 1) * nbl)
    rank = jnp.sum((mine[:, :, None, :] & earlier).astype(jnp.int32), axis=3)
    chosen = mine[:, :, None] & (
        rank[:, :, None] == jnp.arange(CAP, dtype=jnp.int32)[None, None, :, None]
    )
    picked = jnp.max(jnp.where(chosen, (lists % nbl)[:, :, None], -1), axis=3)
    tiles_row = cols // BLOCK
    group_ids = jnp.arange(groups, dtype=jnp.int32)[:, None, None]
    where = (picked % tiles_row) * rows + grows * group_ids + picked // tiles_row
    where = jnp.where(picked >= 0, where, -1).reshape(-1, 1)
    sel = (where == jnp.arange(rows * tiles_row, dtype=jnp.int32)[None]).astype(jnp.bfloat16)
    source = jnp.where(own >= 0, own // nbl, -1)
    same = (source[None, :] == source[:, None]) & earlier
    slots = jnp.where(own >= 0, source * CAP + jnp.sum(same.astype(jnp.int32), axis=1), -1)

    regrouped = (groups, ifgs, nslots, BLOCK)
    w, d = pl.pallas_call(
        spread_kernel,
        in_specs=[vmem] * 7,
        out_specs=[vmem] * 2,
        out_shape=[
            jax.ShapeDtypeStruct(regrouped, jnp.bfloat16),
            jax.ShapeDtypeStruct(regrouped, jnp.int16),
        ],
        scratch_shapes=[pltpu.VMEM(regrouped, jnp.bfloat16), pltpu.VMEM(regrouped, jnp.int16)]
        + [dma((groups,))] * 4
        + [dma((2,))],
        compiler_params=pltpu.CompilerParams(
            collective_id=1, has_side_effects=True, vmem_limit_bytes=48 * 2**20
        ),
        name="spread",
    )(phases, un, us, coherence, cn, cs, sel)

    send = pl.pallas_call(
        solve_kernel,
        in_specs=[smem, vmem, vmem],
        out_specs=vmem,
        out_shape=jax.ShapeDtypeStruct((nslots, padded, BLOCK), jnp.bfloat16),
        scratch_shapes=[
            pltpu.SMEM((SPAN * DATES,), jnp.int32),
            pltpu.VMEM((unknowns, 4, nslots, BLOCK), jnp.float32),
            pltpu.VMEM((padded * nslots, BLOCK), jnp.float32),
        ],
        compiler_params=pltpu.CompilerParams(vmem_limit_bytes=48 * 2**20),
        name="solve",
    )(design, w.reshape(-1, nslots, BLOCK), d.reshape(-1, nslots, BLOCK))

    return pl.pallas_call(
        functools.partial(geo_kernel, width),
        in_specs=[smem, vmem, vmem],
        out_specs=vmem,
        out_shape=jax.ShapeDtypeStruct((tiles, unknowns, geo_weights.shape[3]), jnp.float32),
        scratch_shapes=[
            pltpu.VMEM((nslots, padded, BLOCK), jnp.bfloat16),
            dma((bands,)),
            dma((bands,)),
            dma,
        ],
        compiler_params=pltpu.CompilerParams(
            collective_id=2, has_side_effects=True, vmem_limit_bytes=32 * 2**20
        ),
        name="geo",
    )(slots, send, geo_weights)


def solution(mesh):
    placed = (
        P("ifg", "space", None),
        P("ifg", "space", None),
        P(),
        P(("space", "ifg"), None),
        P(("space", "ifg"), None, None, None),
    )
    return jax.shard_map(
        per_device,
        mesh=mesh,
        in_specs=placed,
        out_specs=P(("space", "ifg"), None, None),
        check_vma=False,
    )
```

```python
import functools
import jax
import jax.numpy as jnp
from jax import lax
from jax.experimental import pallas as pl
from jax.experimental.pallas import tpu as pltpu
from jax.sharding import PartitionSpec as P

DATES = 100
SPAN = 3
PASSES = 3
BLOCK = 128
CAP = 2
STEP_SIZE = 0.2
SMOOTHING = 0.3
RIDGE_TERM = 0.2
OCTAVE = 1280.0
FLOOR = 21.9
UNROLL = 4
MESH = pl.DeviceIdType.MESH


def encode(u):
    size = (jnp.log2(jnp.maximum(jnp.abs(u), 1e-30)) + FLOOR) * OCTAVE + 0.5
    code = jnp.clip(size, 0.0, 32767.0).astype(jnp.int32)
    return jnp.where(u < 0, -code, code).astype(jnp.int16)


def decode(code):
    code = code.astype(jnp.int32).astype(jnp.float32)
    size = jnp.exp2(jnp.abs(code) * (1.0 / OCTAVE) - FLOOR)
    return jnp.where(code > 0, size, jnp.where(code < 0, -size, 0.0))


def lists_kernel(own_ref, out, send_z, recv_z, send_s, recv_s, own_sem):
    bands, groups = out.shape[:2]
    band, me = lax.axis_index("space"), lax.axis_index("ifg")
    along = [(band, lax.rem(me + r, groups)) for r in range(1, groups)]
    across = [(lax.rem(band + r, bands), me) for r in range(1, bands)]
    barrier = pltpu.get_barrier_semaphore()
    for peer in along + across:
        pl.semaphore_signal(barrier, inc=1, device_id=peer, device_id_type=MESH)
    pl.semaphore_wait(barrier, groups + bands - 2)
    first = [
        pltpu.make_async_remote_copy(
            src_ref=own_ref,
            dst_ref=out.at[band, pl.ds(me, 1)],
            send_sem=send_z.at[r],
            recv_sem=recv_z.at[r],
            device_id=peer,
            device_id_type=MESH,
        )
        for r, peer in enumerate(along)
    ]
    for copy in first:
        copy.start()
    mine = pltpu.make_async_copy(own_ref, out.at[band, pl.ds(me, 1)], own_sem)
    mine.start()
    mine.wait()
    for copy in first:
        copy.wait()
    second = [
        pltpu.make_async_remote_copy(
            src_ref=out.at[band],
            dst_ref=out.at[band],
            send_sem=send_s.at[r],
            recv_sem=recv_s.at[r],
            device_id=peer,
            device_id_type=MESH,
        )
        for r, peer in enumerate(across)
    ]
    for copy in second:
        copy.start()
    for copy in second:
        copy.wait()


def spread_kernel(
    u_ref, c_ref, sel_ref, w_out, d_out, w_send, d_send, up_send, down_send, south, north,
    send_w, recv_w, send_d, recv_d, send_up, recv_up, send_down, recv_down, own_sem,
):
    band = lax.axis_index("space")
    last = lax.axis_size("space") - 1
    me = lax.axis_index("ifg")
    groups = lax.axis_size("ifg")
    ifgs, rows, cols = u_ref.shape
    slots = w_out.shape[2]
    barrier = pltpu.get_barrier_semaphore()
    peers = [lax.rem(me + r, groups) for r in range(groups)]
    for r in range(1, groups):
        pl.semaphore_signal(barrier, inc=1, device_id=(band, peers[r]), device_id_type=MESH)

    @pl.when(band > 0)
    def _():
        pl.semaphore_signal(barrier, inc=1, device_id=(band - 1, me), device_id_type=MESH)

    @pl.when(band < last)
    def _():
        pl.semaphore_signal(barrier, inc=1, device_id=(band + 1, me), device_id_type=MESH)

    beside = (band > 0).astype(jnp.int32) + (band < last).astype(jnp.int32)
    pl.semaphore_wait(barrier, groups - 1 + beside)

    def shift(i, src, dst, send_sem, recv_sem, to):
        return pltpu.make_async_remote_copy(
            src_ref=src.at[i],
            dst_ref=dst.at[i],
            send_sem=send_sem.at[i],
            recv_sem=recv_sem.at[i],
            device_id=(to, me),
            device_id_type=MESH,
        )

    def go_up(i):
        return shift(i, up_send, south, send_up, recv_up, band - 1)

    def go_down(i):
        return shift(i, down_send, north, send_down, recv_down, band + 1)

    @pl.when(band == 0)
    def _():
        north[...] = jnp.zeros_like(north)

    @pl.when(band == last)
    def _():
        south[...] = jnp.zeros_like(south)

    def push(src, dst, span, send_sem, recv_sem, r):
        return pltpu.make_async_remote_copy(
            src_ref=src.at[peers[r], span],
            dst_ref=dst.at[me, span],
            send_sem=send_sem.at[r],
            recv_sem=recv_sem.at[r],
            device_id=(band, peers[r]),
            device_id_type=MESH,
        )

    def tiles(x):
        return jnp.concatenate(
            [x[:, q * BLOCK : (q + 1) * BLOCK] for q in range(cols // BLOCK)], axis=0
        )

    def pick(x):
        return jnp.dot(sel_ref[...], x, preferred_element_type=jnp.float32)

    def weigh(i, _):
        tops, ends = [], []
        for kk in range(UNROLL):
            k = i * UNROLL + kk
            c = c_ref[k]
            got = pick(tiles(c))
            for g in range(groups):
                w_send[g, k] = got[g * slots : (g + 1) * slots].astype(w_send.dtype)
            u, c = u_ref[k], c.astype(jnp.float32)
            tops += [u[:PASSES], c[:PASSES]]
            ends += [u[rows - PASSES :], c[rows - PASSES :]]
        for r in range(1, groups):
            push(w_send, w_out, pl.ds(i * UNROLL, UNROLL), send_w, recv_w, r).start()

        @pl.when(band > 0)
        def _():
            up_send[i] = jnp.concatenate(tops, axis=0)
            go_up(i).start()

        @pl.when(band < last)
        def _():
            down_send[i] = jnp.concatenate(ends, axis=0)
            go_down(i).start()

        return 0

    lax.fori_loop(0, ifgs // UNROLL, weigh, 0)
    everything = pl.ds(0, ifgs)
    own_w = pltpu.make_async_copy(w_send.at[me], w_out.at[me], own_sem.at[0])
    own_w.start()

    total = rows + 8
    row = lax.broadcasted_iota(jnp.int32, (total, cols), 0)
    col = lax.broadcasted_iota(jnp.int32, (total, cols), 1)
    cut = ((row == total - 1) & (band == 0)) | ((row == rows - 1) & (band == last))
    vert = jnp.where(cut, 0.0, 0.5 * STEP_SIZE)
    east = jnp.where(col == cols - 1, 0.0, 0.5 * STEP_SIZE)
    gap = jnp.zeros((2, cols), jnp.float32)

    def diffuse(i, _):
        @pl.when(band > 0)
        def _():
            go_up(i).wait_send()
            go_down(i).wait_recv()

        @pl.when(band < last)
        def _():
            go_down(i).wait_send()
            go_up(i).wait_recv()

        above, below = north[i], south[i]
        for kk in range(UNROLL):
            k = i * UNROLL + kk
            a = 2 * PASSES * kk
            b, e = a + PASSES, a + 2 * PASSES
            u = jnp.concatenate([u_ref[k], below[a:b], gap, above[a:b]], axis=0)
            c = jnp.concatenate(
                [c_ref[k].astype(jnp.float32), below[b:e], gap, above[b:e]], axis=0
            )
            cv = vert * (c + pltpu.roll(c, total - 1, 0))
            ce = east * (c + pltpu.roll(c, cols - 1, 1))
            for _ in range(PASSES):
                dv = pltpu.roll(u, total - 1, 0) - u
                de = pltpu.roll(u, cols - 1, 1) - u
                fv = cv * dv / (1.0 + 0.25 * (dv * dv))
                fe = ce * de / (1.0 + 0.25 * (de * de))
                u = u + ((fv - pltpu.roll(fv, 1, 0)) + (fe - pltpu.roll(fe, 1, 1)))
            u = tiles(u[:rows])
            high = u.astype(jnp.bfloat16)
            got = pick(high) + pick((u - high.astype(jnp.float32)).astype(jnp.bfloat16))
            for g in range(groups):
                d_send[g, k] = encode(got[g * slots : (g + 1) * slots])
        for r in range(1, groups):
            push(d_send, d_out, pl.ds(i * UNROLL, UNROLL), send_d, recv_d, r).start()
        return 0

    lax.fori_loop(0, ifgs // UNROLL, diffuse, 0)
    own_d = pltpu.make_async_copy(d_send.at[me], d_out.at[me], own_sem.at[1])
    own_d.start()
    own_w.wait()
    own_d.wait()
    for r in range(1, groups):
        push(w_send, w_out, everything, send_w, recv_w, r).wait()
        push(d_send, d_out, everything, send_d, recv_d, r).wait()


def solve_kernel(
    width, table, slots, w_ref, d_ref, weights, out, low, total, send, blocks,
    send_sem, recv_sem, own_sem,
):
    _, subs, lanes = w_ref.shape
    unknowns = DATES - 1
    padded = send.shape[1]
    bands = lax.axis_size("space")
    me = lax.axis_index("space")
    group = lax.axis_index("ifg")
    barrier = pltpu.get_barrier_semaphore()
    peers = [lax.rem(me + r, bands) for r in range(bands)]
    for r in range(1, bands):
        pl.semaphore_signal(barrier, inc=1, device_id=(peers[r], group), device_id_type=MESH)

    def load(t):
        ws, wds = [], []
        for s in range(SPAN):
            k = table[s * DATES + t]
            used = k >= 0
            k = jnp.maximum(k, 0)
            w = jnp.where(used, w_ref[k].astype(jnp.float32), 0.0)
            ws.append(w)
            wds.append(w * decode(d_ref[k]))
        return ws, wds

    ws, wds = load(0)
    zero = ws[0] * 0.0

    def step(j, carry):
        d1, d2, d3, e1, e2, f1, b1, b2, b3 = carry
        (w1, w2, w3), (r1, r2, r3) = load(j + 1)
        diag = jnp.where(
            j == unknowns - 1, 1.0, jnp.where((j == 0) | (j == unknowns - 2), 5.0, 6.0)
        )
        first_off = jnp.where(j == unknowns - 2, -2.0, -4.0)
        a0 = d1 + (w1 + w2 + w3) + (SMOOTHING * diag + RIDGE_TERM)
        a1 = e1 - w1 + jnp.where(j == unknowns - 1, 0.0, SMOOTHING * first_off)
        a2 = f1 - w2 + jnp.where(j >= unknowns - 2, 0.0, SMOOTHING)
        a3 = -w3
        b = b1 - (r1 + r2 + r3)
        inv = 1.0 / a0
        l1, l2, l3 = a1 * inv, a2 * inv, a3 * inv
        low[j, 0], low[j, 1], low[j, 2] = l1, l2, l3
        low[j, 3] = b * inv
        return (
            (d2 + w1) - l1 * a1,
            (d3 + w2) - l2 * a2,
            w3 - l3 * a3,
            e2 - l1 * a2,
            -(l2 * a3),
            -(l1 * a3),
            (b2 + r1) - l1 * b,
            (b3 + r2) - l2 * b,
            r3 - l3 * b,
        )

    lax.fori_loop(0, unknowns, step, (*ws, zero, zero, zero, *wds), unroll=3)

    def back(i, carry):
        x1, x2, x3 = carry
        j = unknowns - 1 - i
        x = low[j, 3] - low[j, 2] * x3 - low[j, 1] * x2 - low[j, 0] * x1
        total[pl.ds(pl.multiple_of(j * subs, 8), subs), :] = x
        return x, x1, x2

    total[pl.ds(unknowns * subs, (padded - unknowns) * subs), :] = jnp.zeros(
        ((padded - unknowns) * subs, lanes), jnp.float32
    )
    lax.fori_loop(0, unknowns, back, (zero, zero, zero), unroll=9)
    for s in range(subs):
        send[s] = total[pl.ds(s, padded, stride=subs), :].astype(send.dtype)

    pl.semaphore_wait(barrier, bands - 1)
    copies = [
        pltpu.make_async_remote_copy(
            src_ref=send.at[pl.ds(peers[r] * CAP, CAP)],
            dst_ref=blocks.at[pl.ds(me * CAP, CAP)],
            send_sem=send_sem.at[r],
            recv_sem=recv_sem.at[r],
            device_id=(peers[r], group),
            device_id_type=MESH,
        )
        for r in range(1, bands)
    ]
    for copy in copies:
        copy.start()
    own = pltpu.make_async_copy(
        send.at[pl.ds(me * CAP, CAP)], blocks.at[pl.ds(me * CAP, CAP)], own_sem
    )
    own.start()
    own.wait()
    for copy in copies:
        copy.wait()
    for t in range(out.shape[0]):
        acc = jnp.zeros((blocks.shape[1], out.shape[2]), jnp.float32)
        for j in range(width):
            slot = slots[t * width + j]
            block = blocks[jnp.maximum(slot, 0)]
            block = jnp.where(slot >= 0, block, jnp.zeros_like(block))
            acc = acc + jnp.dot(block, weights[t, j], preferred_element_type=jnp.float32)
        out[t] = acc[: out.shape[1]]


def per_device(phases, coherence, design, geo_lookup, geo_weights):
    bands = lax.axis_size("space")
    groups = lax.axis_size("ifg")
    ifgs, rows, cols = phases.shape
    band = lax.axis_index("space")
    unknowns = DATES - 1
    padded = (unknowns + 15) // 16 * 16
    pixels = rows * cols // groups
    nbl = pixels // BLOCK
    grows = rows // groups
    tiles, width = geo_lookup.shape
    entries = tiles * width
    nslots = bands * CAP
    vmem = pl.BlockSpec(memory_space=pltpu.VMEM)
    smem = pl.BlockSpec(memory_space=pltpu.SMEM)
    dma = pltpu.SemaphoreType.DMA

    own = geo_lookup.reshape(-1)
    lists = pl.pallas_call(
        lists_kernel,
        in_specs=[vmem],
        out_specs=vmem,
        out_shape=jax.ShapeDtypeStruct((bands, groups, 8, BLOCK), jnp.int32),
        scratch_shapes=[dma((groups,))] * 2 + [dma((bands,))] * 2 + [dma],
        compiler_params=pltpu.CompilerParams(collective_id=0, has_side_effects=True),
        name="lists",
    )(jnp.broadcast_to(jnp.pad(own, (0, BLOCK - entries)), (1, 8, BLOCK)))
    lists = lists[:, :, 0, :entries].transpose(1, 0, 2)
    order = jnp.arange(entries, dtype=jnp.int32)
    earlier = order[None, :] < order[:, None]
    mine = (lists >= band * nbl) & (lists < (band + 1) * nbl)
    rank = jnp.sum((mine[:, :, None, :] & earlier).astype(jnp.int32), axis=3)
    chosen = mine[:, :, None] & (
        rank[:, :, None] == jnp.arange(CAP, dtype=jnp.int32)[None, None, :, None]
    )
    picked = jnp.max(jnp.where(chosen, (lists % nbl)[:, :, None], -1), axis=3)
    tiles_row = cols // BLOCK
    group_ids = jnp.arange(groups, dtype=jnp.int32)[:, None, None]
    where = (picked % tiles_row) * rows + grows * group_ids + picked // tiles_row
    where = jnp.where(picked >= 0, where, -1).reshape(-1, 1)
    sel = (where == jnp.arange(rows * tiles_row, dtype=jnp.int32)[None]).astype(jnp.bfloat16)
    source = jnp.where(own >= 0, own // nbl, -1)
    same = (source[None, :] == source[:, None]) & earlier
    slots = jnp.where(own >= 0, source * CAP + jnp.sum(same.astype(jnp.int32), axis=1), -1)

    regrouped = (groups, ifgs, nslots, BLOCK)
    w, d = pl.pallas_call(
        spread_kernel,
        in_specs=[vmem] * 3,
        out_specs=[vmem] * 2,
        out_shape=[
            jax.ShapeDtypeStruct(regrouped, jnp.bfloat16),
            jax.ShapeDtypeStruct(regrouped, jnp.int16),
        ],
        scratch_shapes=[pltpu.VMEM(regrouped, jnp.bfloat16), pltpu.VMEM(regrouped, jnp.int16)]
        + [pltpu.VMEM((ifgs // UNROLL, 2 * PASSES * UNROLL, cols), jnp.float32)] * 4
        + [dma((groups,))] * 4
        + [dma((ifgs // UNROLL,))] * 4
        + [dma((2,))],
        compiler_params=pltpu.CompilerParams(
            collective_id=1, has_side_effects=True, vmem_limit_bytes=48 * 2**20
        ),
        name="spread",
    )(phases, coherence, sel)

    key = (design[:, 1] - design[:, 0] - 1) * DATES + design[:, 0]
    keys = jnp.arange(SPAN * DATES, dtype=jnp.int32)[:, None]
    index = jnp.arange(design.shape[0], dtype=jnp.int32)[None]
    table = jnp.max(jnp.where(key[None] == keys, index, -1), axis=1)

    return pl.pallas_call(
        functools.partial(solve_kernel, width),
        in_specs=[smem, smem, vmem, vmem, vmem],
        out_specs=vmem,
        out_shape=jax.ShapeDtypeStruct((tiles, unknowns, geo_weights.shape[3]), jnp.float32),
        scratch_shapes=[
            pltpu.VMEM((unknowns, 4, nslots, BLOCK), jnp.float32),
            pltpu.VMEM((padded * nslots, BLOCK), jnp.float32),
            pltpu.VMEM((nslots, padded, BLOCK), jnp.bfloat16),
            pltpu.VMEM((nslots, padded, BLOCK), jnp.bfloat16),
            dma((bands,)),
            dma((bands,)),
            dma,
        ],
        compiler_params=pltpu.CompilerParams(
            collective_id=2, has_side_effects=True, vmem_limit_bytes=48 * 2**20
        ),
        name="solve",
    )(
        table,
        slots,
        w.reshape(-1, nslots, BLOCK),
        d.reshape(-1, nslots, BLOCK),
        geo_weights,
    )


def solution(mesh):
    placed = (
        P("ifg", "space", None),
        P("ifg", "space", None),
        P(),
        P(("space", "ifg"), None),
        P(("space", "ifg"), None, None, None),
    )
    return jax.shard_map(
        per_device,
        mesh=mesh,
        in_specs=placed,
        out_specs=P(("space", "ifg"), None, None),
        check_vma=False,
    )
```

```python
import functools
import jax
import jax.numpy as jnp
from jax import lax
from jax.experimental import pallas as pl
from jax.experimental.pallas import tpu as pltpu
from jax.sharding import PartitionSpec as P

DATES = 100
SPAN = 3
PASSES = 3
BLOCK = 128
CAP = 2
STEP_SIZE = 0.2
SMOOTHING = 0.3
RIDGE_TERM = 0.2
OCTAVE = 1280.0
FLOOR = 21.9
UNROLL = 4
MESH = pl.DeviceIdType.MESH


def encode(u):
    size = (jnp.log2(jnp.maximum(jnp.abs(u), 1e-30)) + FLOOR) * OCTAVE + 0.5
    code = jnp.clip(size, 0.0, 32767.0).astype(jnp.int32)
    return jnp.where(u < 0, -code, code).astype(jnp.int16)


def decode(code):
    code = code.astype(jnp.int32).astype(jnp.float32)
    size = jnp.exp2(jnp.abs(code) * (1.0 / OCTAVE) - FLOOR)
    return jnp.where(code > 0, size, jnp.where(code < 0, -size, 0.0))


def lists_kernel(own_ref, out, send_z, recv_z, send_s, recv_s, own_sem):
    bands, groups = out.shape[:2]
    band, me = lax.axis_index("space"), lax.axis_index("ifg")
    along = [(band, lax.rem(me + r, groups)) for r in range(1, groups)]
    across = [(lax.rem(band + r, bands), me) for r in range(1, bands)]
    barrier = pltpu.get_barrier_semaphore()
    for peer in along + across:
        pl.semaphore_signal(barrier, inc=1, device_id=peer, device_id_type=MESH)
    pl.semaphore_wait(barrier, groups + bands - 2)
    first = [
        pltpu.make_async_remote_copy(
            src_ref=own_ref,
            dst_ref=out.at[band, pl.ds(me, 1)],
            send_sem=send_z.at[r],
            recv_sem=recv_z.at[r],
            device_id=peer,
            device_id_type=MESH,
        )
        for r, peer in enumerate(along)
    ]
    for copy in first:
        copy.start()
    mine = pltpu.make_async_copy(own_ref, out.at[band, pl.ds(me, 1)], own_sem)
    mine.start()
    mine.wait()
    for copy in first:
        copy.wait()
    second = [
        pltpu.make_async_remote_copy(
            src_ref=out.at[band],
            dst_ref=out.at[band],
            send_sem=send_s.at[r],
            recv_sem=recv_s.at[r],
            device_id=peer,
            device_id_type=MESH,
        )
        for r, peer in enumerate(across)
    ]
    for copy in second:
        copy.start()
    for copy in second:
        copy.wait()


def spread_kernel(
    u_ref, c_ref, sel_ref, w_out, d_out, w_send, d_send, up_send, down_send, south, north,
    send_w, recv_w, send_d, recv_d, send_up, recv_up, send_down, recv_down, own_sem,
):
    band = lax.axis_index("space")
    last = lax.axis_size("space") - 1
    me = lax.axis_index("ifg")
    groups = lax.axis_size("ifg")
    ifgs, rows, cols = u_ref.shape
    slots = w_out.shape[2]
    barrier = pltpu.get_barrier_semaphore()
    peers = [lax.rem(me + r, groups) for r in range(groups)]
    for r in range(1, groups):
        pl.semaphore_signal(barrier, inc=1, device_id=(band, peers[r]), device_id_type=MESH)

    @pl.when(band > 0)
    def _():
        pl.semaphore_signal(barrier, inc=1, device_id=(band - 1, me), device_id_type=MESH)

    @pl.when(band < last)
    def _():
        pl.semaphore_signal(barrier, inc=1, device_id=(band + 1, me), device_id_type=MESH)

    beside = (band > 0).astype(jnp.int32) + (band < last).astype(jnp.int32)
    pl.semaphore_wait(barrier, groups - 1 + beside)

    def shift(i, src, dst, send_sem, recv_sem, to):
        return pltpu.make_async_remote_copy(
            src_ref=src.at[i],
            dst_ref=dst.at[i],
            send_sem=send_sem.at[i],
            recv_sem=recv_sem.at[i],
            device_id=(to, me),
            device_id_type=MESH,
        )

    def go_up(i):
        return shift(i, up_send, south, send_up, recv_up, band - 1)

    def go_down(i):
        return shift(i, down_send, north, send_down, recv_down, band + 1)

    @pl.when(band == 0)
    def _():
        north[...] = jnp.zeros_like(north)

    @pl.when(band == last)
    def _():
        south[...] = jnp.zeros_like(south)

    def push(src, dst, span, send_sem, recv_sem, r):
        return pltpu.make_async_remote_copy(
            src_ref=src.at[peers[r], span],
            dst_ref=dst.at[me, span],
            send_sem=send_sem.at[r],
            recv_sem=recv_sem.at[r],
            device_id=(band, peers[r]),
            device_id_type=MESH,
        )

    def tiles(x):
        return jnp.concatenate(
            [x[:, q * BLOCK : (q + 1) * BLOCK] for q in range(cols // BLOCK)], axis=0
        )

    def pick(x):
        return jnp.dot(sel_ref[...], x, preferred_element_type=jnp.float32)

    def weigh(i, _):
        tops, ends = [], []
        for kk in range(UNROLL):
            k = i * UNROLL + kk
            c = c_ref[k]
            got = pick(tiles(c))
            for g in range(groups):
                w_send[g, k] = got[g * slots : (g + 1) * slots].astype(w_send.dtype)
            u, c = u_ref[k], c.astype(jnp.float32)
            tops += [u[:PASSES], c[:PASSES]]
            ends += [u[rows - PASSES :], c[rows - PASSES :]]
        for r in range(1, groups):
            push(w_send, w_out, pl.ds(i * UNROLL, UNROLL), send_w, recv_w, r).start()

        @pl.when(band > 0)
        def _():
            up_send[i] = jnp.concatenate(tops, axis=0)
            go_up(i).start()

        @pl.when(band < last)
        def _():
            down_send[i] = jnp.concatenate(ends, axis=0)
            go_down(i).start()

        return 0

    lax.fori_loop(0, ifgs // UNROLL, weigh, 0)
    everything = pl.ds(0, ifgs)
    own_w = pltpu.make_async_copy(w_send.at[me], w_out.at[me], own_sem.at[0])
    own_w.start()

    total = rows + 8
    row = lax.broadcasted_iota(jnp.int32, (total, cols), 0)
    col = lax.broadcasted_iota(jnp.int32, (total, cols), 1)
    cut = ((row == total - 1) & (band == 0)) | ((row == rows - 1) & (band == last))
    vert = jnp.where(cut, 0.0, 0.5 * STEP_SIZE)
    east = jnp.where(col == cols - 1, 0.0, 0.5 * STEP_SIZE)
    gap = jnp.zeros((2, cols), jnp.float32)

    def diffuse(i, _):
        @pl.when(band > 0)
        def _():
            go_up(i).wait_send()
            go_down(i).wait_recv()

        @pl.when(band < last)
        def _():
            go_down(i).wait_send()
            go_up(i).wait_recv()

        above, below = north[i], south[i]
        for kk in range(UNROLL):
            k = i * UNROLL + kk
            a = 2 * PASSES * kk
            b, e = a + PASSES, a + 2 * PASSES
            u = jnp.concatenate([u_ref[k], below[a:b], gap, above[a:b]], axis=0)
            c = jnp.concatenate(
                [c_ref[k].astype(jnp.float32), below[b:e], gap, above[b:e]], axis=0
            )
            cv = vert * (c + pltpu.roll(c, total - 1, 0))
            ce = east * (c + pltpu.roll(c, cols - 1, 1))
            for _ in range(PASSES):
                dv = pltpu.roll(u, total - 1, 0) - u
                de = pltpu.roll(u, cols - 1, 1) - u
                av = 1.0 + 0.25 * (dv * dv)
                ae = 1.0 + 0.25 * (de * de)
                both = av * ae
                inv = pl.reciprocal(both, approx=True)
                inv = inv * (2.0 - both * inv)
                fv = cv * dv * (ae * inv)
                fe = ce * de * (av * inv)
                u = u + ((fv - pltpu.roll(fv, 1, 0)) + (fe - pltpu.roll(fe, 1, 1)))
            u = tiles(u[:rows])
            high = u.astype(jnp.bfloat16)
            got = pick(high) + pick((u - high.astype(jnp.float32)).astype(jnp.bfloat16))
            for g in range(groups):
                d_send[g, k] = encode(got[g * slots : (g + 1) * slots])
        for r in range(1, groups):
            push(d_send, d_out, pl.ds(i * UNROLL, UNROLL), send_d, recv_d, r).start()
        return 0

    lax.fori_loop(0, ifgs // UNROLL, diffuse, 0)
    own_d = pltpu.make_async_copy(d_send.at[me], d_out.at[me], own_sem.at[1])
    own_d.start()
    own_w.wait()
    own_d.wait()
    for r in range(1, groups):
        push(w_send, w_out, everything, send_w, recv_w, r).wait()
        push(d_send, d_out, everything, send_d, recv_d, r).wait()


def solve_kernel(
    width, table, slots, w_ref, d_ref, weights, out, low, total, send, blocks,
    send_sem, recv_sem, own_sem,
):
    _, subs, lanes = w_ref.shape
    unknowns = DATES - 1
    padded = send.shape[1]
    bands = lax.axis_size("space")
    me = lax.axis_index("space")
    group = lax.axis_index("ifg")
    barrier = pltpu.get_barrier_semaphore()
    peers = [lax.rem(me + r, bands) for r in range(bands)]
    for r in range(1, bands):
        pl.semaphore_signal(barrier, inc=1, device_id=(peers[r], group), device_id_type=MESH)

    def load(t):
        ws, wds = [], []
        for s in range(SPAN):
            k = table[s * DATES + t]
            used = k >= 0
            k = jnp.maximum(k, 0)
            w = jnp.where(used, w_ref[k].astype(jnp.float32), 0.0)
            ws.append(w)
            wds.append(w * decode(d_ref[k]))
        return ws, wds

    ws, wds = load(0)
    zero = ws[0] * 0.0

    def step(j, carry):
        d1, d2, d3, e1, e2, f1, b1, b2, b3 = carry
        (w1, w2, w3), (r1, r2, r3) = load(j + 1)
        diag = jnp.where(
            j == unknowns - 1, 1.0, jnp.where((j == 0) | (j == unknowns - 2), 5.0, 6.0)
        )
        first_off = jnp.where(j == unknowns - 2, -2.0, -4.0)
        a0 = d1 + (w1 + w2 + w3) + (SMOOTHING * diag + RIDGE_TERM)
        a1 = e1 - w1 + jnp.where(j == unknowns - 1, 0.0, SMOOTHING * first_off)
        a2 = f1 - w2 + jnp.where(j >= unknowns - 2, 0.0, SMOOTHING)
        a3 = -w3
        b = b1 - (r1 + r2 + r3)
        inv = 1.0 / a0
        l1, l2, l3 = a1 * inv, a2 * inv, a3 * inv
        low[j, 0], low[j, 1], low[j, 2] = l1, l2, l3
        low[j, 3] = b * inv
        return (
            (d2 + w1) - l1 * a1,
            (d3 + w2) - l2 * a2,
            w3 - l3 * a3,
            e2 - l1 * a2,
            -(l2 * a3),
            -(l1 * a3),
            (b2 + r1) - l1 * b,
            (b3 + r2) - l2 * b,
            r3 - l3 * b,
        )

    lax.fori_loop(0, unknowns, step, (*ws, zero, zero, zero, *wds), unroll=3)

    def back(i, carry):
        x1, x2, x3 = carry
        j = unknowns - 1 - i
        x = low[j, 3] - low[j, 2] * x3 - low[j, 1] * x2 - low[j, 0] * x1
        total[pl.ds(pl.multiple_of(j * subs, 8), subs), :] = x
        return x, x1, x2

    total[pl.ds(unknowns * subs, (padded - unknowns) * subs), :] = jnp.zeros(
        ((padded - unknowns) * subs, lanes), jnp.float32
    )
    lax.fori_loop(0, unknowns, back, (zero, zero, zero), unroll=9)
    for s in range(subs):
        send[s] = total[pl.ds(s, padded, stride=subs), :].astype(send.dtype)

    pl.semaphore_wait(barrier, bands - 1)
    copies = [
        pltpu.make_async_remote_copy(
            src_ref=send.at[pl.ds(peers[r] * CAP, CAP)],
            dst_ref=blocks.at[pl.ds(me * CAP, CAP)],
            send_sem=send_sem.at[r],
            recv_sem=recv_sem.at[r],
            device_id=(peers[r], group),
            device_id_type=MESH,
        )
        for r in range(1, bands)
    ]
    for copy in copies:
        copy.start()
    own = pltpu.make_async_copy(
        send.at[pl.ds(me * CAP, CAP)], blocks.at[pl.ds(me * CAP, CAP)], own_sem
    )
    own.start()
    own.wait()
    for copy in copies:
        copy.wait()
    for t in range(out.shape[0]):
        acc = jnp.zeros((blocks.shape[1], out.shape[2]), jnp.float32)
        for j in range(width):
            slot = slots[t * width + j]
            block = blocks[jnp.maximum(slot, 0)]
            block = jnp.where(slot >= 0, block, jnp.zeros_like(block))
            acc = acc + jnp.dot(block, weights[t, j], preferred_element_type=jnp.float32)
        out[t] = acc[: out.shape[1]]


def per_device(phases, coherence, design, geo_lookup, geo_weights):
    bands = lax.axis_size("space")
    groups = lax.axis_size("ifg")
    ifgs, rows, cols = phases.shape
    band = lax.axis_index("space")
    unknowns = DATES - 1
    padded = (unknowns + 15) // 16 * 16
    pixels = rows * cols // groups
    nbl = pixels // BLOCK
    grows = rows // groups
    tiles, width = geo_lookup.shape
    entries = tiles * width
    nslots = bands * CAP
    vmem = pl.BlockSpec(memory_space=pltpu.VMEM)
    smem = pl.BlockSpec(memory_space=pltpu.SMEM)
    dma = pltpu.SemaphoreType.DMA

    own = geo_lookup.reshape(-1)
    lists = pl.pallas_call(
        lists_kernel,
        in_specs=[vmem],
        out_specs=vmem,
        out_shape=jax.ShapeDtypeStruct((bands, groups, 8, BLOCK), jnp.int32),
        scratch_shapes=[dma((groups,))] * 2 + [dma((bands,))] * 2 + [dma],
        compiler_params=pltpu.CompilerParams(collective_id=0, has_side_effects=True),
        name="lists",
    )(jnp.broadcast_to(jnp.pad(own, (0, BLOCK - entries)), (1, 8, BLOCK)))
    lists = lists[:, :, 0, :entries].transpose(1, 0, 2)
    order = jnp.arange(entries, dtype=jnp.int32)
    earlier = order[None, :] < order[:, None]
    mine = (lists >= band * nbl) & (lists < (band + 1) * nbl)
    rank = jnp.sum((mine[:, :, None, :] & earlier).astype(jnp.int32), axis=3)
    chosen = mine[:, :, None] & (
        rank[:, :, None] == jnp.arange(CAP, dtype=jnp.int32)[None, None, :, None]
    )
    picked = jnp.max(jnp.where(chosen, (lists % nbl)[:, :, None], -1), axis=3)
    tiles_row = cols // BLOCK
    group_ids = jnp.arange(groups, dtype=jnp.int32)[:, None, None]
    where = (picked % tiles_row) * rows + grows * group_ids + picked // tiles_row
    where = jnp.where(picked >= 0, where, -1).reshape(-1, 1)
    sel = (where == jnp.arange(rows * tiles_row, dtype=jnp.int32)[None]).astype(jnp.bfloat16)
    source = jnp.where(own >= 0, own // nbl, -1)
    same = (source[None, :] == source[:, None]) & earlier
    slots = jnp.where(own >= 0, source * CAP + jnp.sum(same.astype(jnp.int32), axis=1), -1)

    regrouped = (groups, ifgs, nslots, BLOCK)
    w, d = pl.pallas_call(
        spread_kernel,
        in_specs=[vmem] * 3,
        out_specs=[vmem] * 2,
        out_shape=[
            jax.ShapeDtypeStruct(regrouped, jnp.bfloat16),
            jax.ShapeDtypeStruct(regrouped, jnp.int16),
        ],
        scratch_shapes=[pltpu.VMEM(regrouped, jnp.bfloat16), pltpu.VMEM(regrouped, jnp.int16)]
        + [pltpu.VMEM((ifgs // UNROLL, 2 * PASSES * UNROLL, cols), jnp.float32)] * 4
        + [dma((groups,))] * 4
        + [dma((ifgs // UNROLL,))] * 4
        + [dma((2,))],
        compiler_params=pltpu.CompilerParams(
            collective_id=1, has_side_effects=True, vmem_limit_bytes=48 * 2**20
        ),
        name="spread",
    )(phases, coherence, sel)

    key = (design[:, 1] - design[:, 0] - 1) * DATES + design[:, 0]
    keys = jnp.arange(SPAN * DATES, dtype=jnp.int32)[:, None]
    index = jnp.arange(design.shape[0], dtype=jnp.int32)[None]
    table = jnp.max(jnp.where(key[None] == keys, index, -1), axis=1)

    return pl.pallas_call(
        functools.partial(solve_kernel, width),
        in_specs=[smem, smem, vmem, vmem, vmem],
        out_specs=vmem,
        out_shape=jax.ShapeDtypeStruct((tiles, unknowns, geo_weights.shape[3]), jnp.float32),
        scratch_shapes=[
            pltpu.VMEM((unknowns, 4, nslots, BLOCK), jnp.float32),
            pltpu.VMEM((padded * nslots, BLOCK), jnp.float32),
            pltpu.VMEM((nslots, padded, BLOCK), jnp.bfloat16),
            pltpu.VMEM((nslots, padded, BLOCK), jnp.bfloat16),
            dma((bands,)),
            dma((bands,)),
            dma,
        ],
        compiler_params=pltpu.CompilerParams(
            collective_id=2, has_side_effects=True, vmem_limit_bytes=48 * 2**20
        ),
        name="solve",
    )(
        table,
        slots,
        w.reshape(-1, nslots, BLOCK),
        d.reshape(-1, nslots, BLOCK),
        geo_weights,
    )


def solution(mesh):
    placed = (
        P("ifg", "space", None),
        P("ifg", "space", None),
        P(),
        P(("space", "ifg"), None),
        P(("space", "ifg"), None, None, None),
    )
    return jax.shard_map(
        per_device,
        mesh=mesh,
        in_specs=placed,
        out_specs=P(("space", "ifg"), None, None),
        check_vma=False,
    )
```
